512 devices in a mesh: mem: 16 (over y_lo, z), sp: 32 (over y_hi, x, core).
Axes of the slice: x: 4, y: 8 (y_hi: 4, y_lo: 2; y = y_hi * 2 + y_lo), z: 8, core: 2. Of those that a mesh axis runs over, the one named last changes fastest.
Arguments:
- grad_image: bfloat16 [16, 256, 128, 512], P('mem', 'sp'), may hold values from -6 to 6
- conv_weight: bfloat16 [3, 3, 512, 512], P(None, None, 'sp', 'mem'), may hold values from -0.09375 to 0.09375
- input_weight: bfloat16 [3, 3, 16, 512], P(None, None, None, 'sp'), may hold values from -0.09375 to 0.09375
- hidden: bfloat16 [16, 2048, 2432], P('mem', 'sp'), may hold values from -6 to 6
- shift: float32 [16, 2432], P('mem'), may hold values from -3 to 3
- scale: float32 [16, 2432], P('mem'), may hold values from -3 to 3
- final_weight: bfloat16 [2432, 64], P('sp'), may hold values from -0.75 to 0.75
Outputs:
- grad_hidden: bfloat16 [16, 2048, 2432], P('mem', 'sp')
- grad_final: float32 [2432, 64], P('sp')
- grad_scale: float32 [16, 2432], P('mem')
- grad_shift: float32 [16, 2432], P('mem')
The draws below stay inside these ranges and needn't reach their ends.
All inputs are finite; a program needn't handle non-finite values.
Results may differ from the reference program's by a relative error of at most 0.011.
Values may be sent and summed in bfloat16 or wider, within the bound.
A program may use at most 64 MiB of HBM per device.

```python
import jax
import jax.numpy as jnp
from jax import lax

C = 512
LAT = 16
D = 2432
COLS = 128
PATCH_OUT = 64
MEMBERS = 16
ROWS = 256
TOKENS = 2048


def steps_of(own_key, shape, shards, low, largest):
    loudness, own = 1.0, jax.random.fold_in(own_key, 6)
    for position, parts in shards:
        heights = jnp.exp(jax.random.uniform(jax.random.fold_in(own, position), (parts,), jnp.float32, low / len(shards), largest / len(shards)))
        loudness = loudness * jnp.repeat(heights, shape[position] // parts).reshape([-1 if axis == position else 1 for axis in range(len(shape))])
    return loudness


def normal_values(stream_key, shape, scale, bound, shards=(), kind=jnp.bfloat16):
    drawn = scale * jax.random.normal(stream_key, shape, jnp.float32)
    if shards:
        drawn = drawn * steps_of(stream_key, shape, shards, -0.22, 0.18)
    return jnp.clip(drawn, -bound, bound).astype(kind)


def setup_inputs(seed: int = 0) -> dict:
    seeds = jax.random.split(jax.random.key(seed), 8)
    return {
        "grad_image": normal_values(seeds[0], (MEMBERS, ROWS, COLS, C), 1.0, 6.0, ((0, 16), (1, 32))),
        "conv_weight": normal_values(seeds[1], (3, 3, C, C), (9 * C) ** -0.5, 0.09375, ((2, 32), (3, 16))),
        "input_weight": normal_values(seeds[2], (3, 3, LAT, C), (9 * C) ** -0.5, 0.09375, ((3, 32),)),
        "hidden": normal_values(seeds[3], (MEMBERS, TOKENS, D), 1.0, 6.0, ((0, 16), (1, 32))),
        "shift": normal_values(seeds[4], (MEMBERS, D), 0.5, 3.0, ((0, 16),), jnp.float32),
        "scale": normal_values(seeds[5], (MEMBERS, D), 0.5, 3.0, ((0, 16),), jnp.float32),
        "final_weight": normal_values(seeds[6], (D, PATCH_OUT), PATCH_OUT ** -0.5, 0.75, ((0, 32),)),
    }


def adjoint_kernel(weight):
    return jnp.transpose(jnp.flip(weight, (0, 1)), (0, 1, 3, 2))

def convolve(field, kernel):
    return lax.conv_general_dilated(field, kernel, (1, 1), 'SAME', dimension_numbers=('NHWC', 'HWIO', 'NHWC'), preferred_element_type=jnp.float32)

def convolve_exact(field, kernel):
    return lax.conv_general_dilated(field, kernel, (1, 1), 'SAME', dimension_numbers=('NHWC', 'HWIO', 'NHWC'), precision=lax.Precision.HIGHEST)

def reference(grad_image, conv_weight, input_weight, hidden, shift, scale, final_weight):
    first_kernel = adjoint_kernel(conv_weight)
    second_kernel = adjoint_kernel(input_weight).astype(jnp.float32)

    def member(items):
        image, hid, shift_row, scale_row = items
        grad_conv = convolve(image[None], first_kernel)
        pooled = grad_conv.reshape(1, ROWS // 2, 2, COLS // 2, 2, C).sum(axis=(2, 4))
        grad_latent = convolve_exact(pooled, second_kernel) / 1.5305
        grad_tokens = grad_latent.reshape(ROWS // 4, 2, COLS // 4, 2, LAT).transpose(0, 2, 1, 3, 4)
        grad_tokens = grad_tokens.reshape(TOKENS, PATCH_OUT).astype(jnp.bfloat16)
        values = hid.astype(jnp.float32)
        centred = values - lax.optimization_barrier(jnp.mean(values, axis=-1, keepdims=True))
        inverse = lax.rsqrt(lax.optimization_barrier(jnp.mean(centred * centred, axis=-1, keepdims=True)) + 1e-06)
        normed = centred * inverse
        modulated = (normed * (1.0 + scale_row) + shift_row).astype(jnp.bfloat16)
        grad_mod = jnp.dot(grad_tokens, final_weight.T, preferred_element_type=jnp.float32)
        grad_shift = lax.optimization_barrier(jnp.sum(grad_mod, axis=0))
        grad_scale = lax.optimization_barrier(jnp.sum(grad_mod * normed, axis=0))
        term = jnp.dot(modulated.T, grad_tokens, preferred_element_type=jnp.float32)
        scaled = grad_mod * (1.0 + scale_row)
        grad_hidden = (scaled - lax.optimization_barrier(jnp.mean(scaled, axis=-1, keepdims=True)) - normed * lax.optimization_barrier(jnp.mean(scaled * normed, axis=-1, keepdims=True))) * inverse
        return (grad_hidden.astype(jnp.bfloat16), grad_scale, grad_shift, term)
    grad_hidden, grad_scale, grad_shift, terms = lax.map(member, (grad_image, hidden, shift, scale))
    return (grad_hidden, lax.optimization_barrier(jnp.sum(terms, axis=0)), grad_scale, grad_shift)
```

```python
import jax
import jax.numpy as jnp
from jax import lax
from jax.experimental import pallas as pl
from jax.experimental.pallas import tpu as pltpu
from jax.sharding import PartitionSpec as P

MESH = pl.DeviceIdType.MESH
F32, BF16 = jnp.float32, jnp.bfloat16
OWNERS = (0, 2, 5, 12, 15)


def iota(shape, dim):
    return lax.broadcasted_iota(jnp.int32, shape, dim)


def kernel(
    g_hbm, cw_ref, iw_ref, hid_hbm, shift_ref, scale_ref, wf_ref,
    gh_ref, gf_ref, gs_ref, gsh_ref,
    gall, hall, kp0, kp1, rsb0, rsb1, kb0, kb1, sx, ps, rhs, zacc, lat, tp, tpr, halo,
    wfb, wff, nrm, inv, ntf, nt2, gtd, nch, nrb, gsp, gsb, cm, mrb, mab,
    ssem, lsem, rs0, rs1, rz0, rz1, ry0, ry1, rx0, rx1, rg, rh, rwy, rwx, rwc, rt, rup, rdn, rn, rgs, rm1, rm2,
):
    mem, sp = lax.axis_index("mem"), lax.axis_index("sp")
    ylo, z = mem // 8, mem % 8
    core, j = sp % 2, sp // 2
    yhi, x = j // 4, j % 4
    other = 1 - core
    pending = []

    def send(src, dst, recv, device, cond=None):
        copy = pltpu.make_async_remote_copy(
            src_ref=src, dst_ref=dst, send_sem=ssem.at[len(pending)], recv_sem=recv,
            device_id=device, device_id_type=MESH,
        )
        pending.append((copy, cond))
        if cond is None:
            copy.start()
        else:
            pl.when(cond)(copy.start)

    def arrived(ref, sem):
        pltpu.make_async_copy(ref, ref, sem).wait()

    barrier = pltpu.get_barrier_semaphore()

    def greet_sp(step, carry):
        pl.semaphore_signal(barrier, inc=1, device_id=(mem, (sp + step) % 32), device_id_type=MESH)
        return carry

    def greet_mem(step, carry):
        pl.semaphore_signal(barrier, inc=1, device_id=((mem + step) % 16, sp), device_id_type=MESH)
        return carry

    def greet_cross(step, carry):
        there = (((yhi + step) % 4) * 4 + x) * 2 + core
        pl.semaphore_signal(barrier, inc=1, device_id=((1 - ylo) * 8 + z, there), device_id_type=MESH)
        return carry

    lax.fori_loop(1, 32, greet_sp, 0)
    lax.fori_loop(1, 16, greet_mem, 0)
    lax.fori_loop(1, 4, greet_cross, 0)

    own_g = pltpu.make_async_copy(
        g_hbm.at[0, :, :, pl.ds(pl.multiple_of(core * 256, 256), 256)],
        gall.at[pl.ds(core * 8, 8)], lsem.at[0])
    own_g.start()
    own_h = pltpu.make_async_copy(hid_hbm.at[0], hall.at[core], lsem.at[1])
    own_h.start()

    iw = iw_ref[...]
    both = jnp.concatenate([iw[:128]] + [iw[128:144]] * 8, axis=0)
    cw = jnp.concatenate([cw_ref[k] for k in range(9)], axis=1)
    part = lax.dot_general(cw, both, (((0,), (1,)), ((), ())), preferred_element_type=F32)
    part = part.reshape(18, 16, 256)
    lane16 = iota((16, 128), 1) // 16
    tiles = [part[k, :, :128] for k in range(18)]
    for first in range(0, 24, 8):
        packed = jnp.zeros((16, 128), F32)
        for k in range(first, min(first + 8, 18)):
            packed = jnp.where(lane16 == k - first, part[k, :, 128:], packed)
        tiles.append(packed)
    for t in range(16):
        kp0[t] = tiles[t].astype(BF16)
    for t in range(8):
        kp1[t] = (tiles[16 + t] if t < 5 else jnp.zeros((16, 128), F32)).astype(BF16)

    wf = wf_ref[...].astype(F32)
    wide = jnp.concatenate([wf[:38], wf[38:76]], axis=1)
    wide = jnp.concatenate([wide, jnp.zeros((10, 128), F32)], axis=0)
    wfb[core, yhi, x] = wide.astype(BF16)

    pl.semaphore_wait(barrier, 49)

    for step in range(16):
        there = (j + step) % 16
        target = (mem, there * 2 + ylo)
        if step:
            send(kp0.at[there], rsb0.at[sp], rs0, target)
        else:
            send(kp0.at[there], rsb0.at[sp], rs0, target, core != ylo)

            @pl.when(core == ylo)
            def _():
                pltpu.make_async_copy(kp0.at[j], rsb0.at[sp], rs0).start()

    for step in range(8):
        there = (j + step) % 8
        target = (mem, there * 2 + ylo)
        if step:
            send(kp1.at[there], rsb1.at[sp], rs1, target)
        else:
            mine = jnp.logical_and(core == ylo, j < 8)
            send(kp1.at[there], rsb1.at[sp], rs1, target, jnp.logical_not(mine))

            @pl.when(mine)
            def _():
                pltpu.make_async_copy(kp1.at[j], rsb1.at[sp], rs1).start()

    partner = (mem, j * 2 + other)
    send(g_hbm.at[0, :, :, pl.ds(pl.multiple_of(other * 256, 256), 256)], gall.at[pl.ds(core * 8, 8)], rg, partner)
    send(hid_hbm.at[0], hall.at[core], rh, partner)
    for step in range(1, 4):
        send(wfb.at[core, yhi, x], wfb.at[core, yhi, x], rwy.at[yhi], (mem, (((yhi + step) % 4) * 4 + x) * 2 + core))

    lanes = iota((48, 2432), 1)
    rows = iota((48, 2432), 0)
    hit_a, hit_b = lanes == sp * 76 + rows, lanes == sp * 76 + 38 + rows
    left = iota((48, 128), 1) < 64
    scale, shift = scale_ref[...], shift_ref[...]

    def pick(values):
        a = jnp.sum(jnp.where(hit_a, values, 0.0), axis=1, keepdims=True)
        b = jnp.sum(jnp.where(hit_b, values, 0.0), axis=1, keepdims=True)
        return jnp.where(left, a, b)

    own_scale, own_shift = 1.0 + pick(scale), pick(shift)

    source = core == ylo
    first_half = yhi < 2
    both_slots = jnp.logical_and(source, first_half)

    @pl.when(source)
    def _():
        arrived(rsb0, rs0)
        kb0[j, z] = jnp.sum(rsb0[...].astype(F32), axis=0).astype(BF16)

    @pl.when(both_slots)
    def _():
        arrived(rsb1, rs1)
        kb1[j, z] = jnp.sum(rsb1[...].astype(F32), axis=0).astype(BF16)

    for step in range(1, 8):
        target = (ylo * 8 + (z + step) % 8, sp)
        send(kb0.at[j, z], kb0.at[j, z], rz0, target, source)
        send(kb1.at[j % 8, z], kb1.at[j % 8, z], rz1, target, both_slots)

    @pl.when(source)
    def _():
        arrived(kb0.at[0, pl.ds(0, 7)], rz0)

    @pl.when(both_slots)
    def _():
        arrived(kb1.at[0, pl.ds(0, 7)], rz1)

    for dlo in range(2):
        for step in range(4):
            if dlo + step == 0:
                continue
            there = (((yhi + step) % 4) * 4 + x) * 2 + core
            target = (((ylo + dlo) % 2) * 8 + z, there)
            send(kb0.at[j], kb0.at[j], ry0.at[yhi], target, source)
            send(kb1.at[j % 8], kb1.at[j % 8], ry1.at[yhi % 2], target, both_slots)

    for piece in range(4):
        missing = jnp.logical_not(jnp.logical_and(source, yhi == piece))
        here = piece * 4 + x

        @pl.when(missing)
        def _():
            arrived(kb0.at[here], ry0.at[piece])
            if piece < 2:
                arrived(kb1.at[here], ry1.at[piece])

        for step in range(1, 4):
            target = (mem, (yhi * 4 + (x + step) % 4) * 2 + core)
            send(kb0.at[here], kb0.at[here], rx0, target)
            if piece < 2:
                send(kb1.at[here], kb1.at[here], rx1, target)

    for piece in range(4):
        @pl.when(yhi != piece)
        def _():
            arrived(wfb.at[core, piece, x], rwy.at[piece])
    for step in range(1, 4):
        send(wfb.at[core, :, x], wfb.at[core, :, x], rwx.at[x], (mem, (yhi * 4 + (x + step) % 4) * 2 + core))

    own_g.wait()
    arrived(gall.at[pl.ds(0, 8)], rg)
    sx[pl.ds(0, 64), pl.ds(768, 1536)] = jnp.zeros((64, 1536), BF16)
    sx[pl.ds(576, 64), pl.ds(0, 1536)] = jnp.zeros((64, 1536), BF16)
    for half in range(2):
        ps[half, pl.ds(0, 8), :] = jnp.zeros((8, 128), F32)
        ps[half, pl.ds(136, 8), :] = jnp.zeros((8, 128), F32)

    def columns(start):
        return jnp.concatenate([ps.at[half][pl.ds(start, 64, stride=2), :] for half in range(2)], axis=1)

    for r in range(-1, 16):
        if r == -1:
            pair = gall[0].astype(F32)
        elif r == 15:
            pair = gall[15].astype(F32)
        else:
            pair = gall[r].astype(F32) + gall[r + 1].astype(F32)
        for half in range(2):
            ps[half, pl.ds(8, 128), :] = pair[:, 128 * half : 128 * half + 128]
        before, even, odd, after = columns(7), columns(8), columns(9), columns(10)
        sums = jnp.concatenate([odd + after, even + odd, before + even], axis=1)
        if r % 2 == 0:
            places = ((r // 2, 1),)
        else:
            places = (((r - 1) // 2, 0), ((r + 1) // 2, 2))
        for i, a in places:
            kept = sums
            if i == -1:
                kept = jnp.where(j > 0, sums, 0.0)
            if i == 8:
                kept = jnp.where(j < 15, sums, 0.0)
            sx[pl.ds((i + 1) * 64, 64), pl.ds(a * 768, 768)] = kept.astype(BF16)

    own_h.wait()
    arrived(hall.at[0], rh)
    for k in range(2):
        values = hall[k].astype(F32)
        centred = values - jnp.mean(values, axis=-1, keepdims=True)
        inverse = lax.rsqrt(jnp.mean(centred * centred, axis=-1, keepdims=True) + 1e-06)
        nrm[pl.ds(k * 64, 64), :] = centred * inverse
        inv[pl.ds(k * 64, 64), :] = jnp.broadcast_to(inverse, (64, 128))
    for k in range(19):
        ntf[pl.ds(k * 128, 128), :] = nrm[:, pl.ds(k * 128, 128)].T
    ntf[pl.ds(2432, 16), :] = jnp.zeros((16, 128), F32)
    row = iota((48, 128), 0)
    for k in range(16):
        for h in range(2):
            a = ntf[pl.ds(152 * k + 38 * h, 48), :]
            b = ntf[pl.ds(152 * k + 76 + 38 * h, 48), :]
            v = jnp.where(core == 0, a, b)
            v = jnp.where(row < 38, v, jnp.where(row == 38, 1.0, 0.0))
            nt2[pl.ds((2 * k + h) * 48, 48), :] = v.astype(BF16)

    for piece in range(4):
        @pl.when(x != piece)
        def _():
            arrived(wfb.at[core, :, piece], rwx.at[piece])
    send(wfb.at[core], wfb.at[core], rwc, partner)

    arrived(kb0.at[pl.ds(0, 12)], rx0)
    arrived(kb1.at[pl.ds(0, 6)], rx1)

    def tile(t):
        return kb0[t] if t < 16 else kb1[t - 16]

    group = iota((8, 16, 128), 2) // 16
    for k in range(9):
        main, last = [], []
        for h in range(2):
            t = 2 * k + h
            main.append(tile(t))
            packed = tile(18 + t // 8)
            last.append(jnp.where(group == t % 8, packed, jnp.zeros_like(packed)))
        pieces = []
        for zz in range(8):
            for h in range(2):
                pieces.append(jnp.concatenate([main[h][zz], last[h][zz]], axis=1))
        rhs[pl.ds(k * 256, 256), :] = jnp.concatenate(pieces, axis=0)

    zacc[...] = jnp.dot(sx[...], rhs[...], preferred_element_type=F32)

    field, corner = zacc[:, :128], zacc[:, 128:]
    column = iota((640, 128), 0) % 64
    g8 = iota((640, 128), 1) // 16
    tap_r, tap_c = g8 // 3, g8 % 3
    minus = jnp.where(column == 63, 0.0, pltpu.roll(field, 639, axis=0))
    plus = jnp.where(column == 0, 0.0, pltpu.roll(field, 1, axis=0))
    corner = jnp.where(column == 0, 0.0, pltpu.roll(corner, 1, axis=0))
    moved = jnp.where(tap_c == 0, minus, jnp.where(tap_c == 1, field, plus))
    none = jnp.zeros((64, 128), F32)
    total = jnp.concatenate([jnp.where(tap_r == 0, moved, 0.0), none, none], axis=0)
    total += jnp.concatenate([none, jnp.where(tap_r == 1, moved, 0.0), none], axis=0)
    total += jnp.concatenate([none, none, jnp.where(tap_r == 2, moved, 0.0) + corner], axis=0)
    total += pltpu.roll(total, 64, axis=1)
    total += pltpu.roll(total, 32, axis=1)
    total += pltpu.roll(total, 16, axis=1)
    lat[...] = total * (1.0 / 1.5305)
    g4 = (iota((32, 128), 1) // 16) % 4
    for r in range(6):
        value = jnp.zeros((32, 128), F32)
        for p in range(2):
            for s in range(2):
                value = jnp.where(g4 == 2 * p + s, lat[pl.ds((2 * r + p) * 64 + s, 32, stride=2), :], value)
        tp[r] = value

    send(tp.at[pl.ds(1, 4)], tpr, rt, partner)
    for c in range(2):
        send(tp.at[0], halo.at[1, core], rdn, (mem, jnp.maximum(2 * j - 2 + c, 0)), j > 0)
        send(tp.at[5], halo.at[0, core], rup, (mem, jnp.minimum(2 * j + 2 + c, 31)), j < 15)

    @pl.when(j == 0)
    def _():
        halo[0] = jnp.zeros((2, 32, 128), F32)

    @pl.when(j == 15)
    def _():
        halo[1] = jnp.zeros((2, 32, 128), F32)

    arrived(wfb.at[0], rwc)
    left = iota((48, 128), 1) < 64
    for k in range(16):
        for c in range(2):
            block = wfb[c, k // 4, k % 4].astype(F32)
            at = 76 * (2 * k + c)
            wff[pl.ds(at, 40), :] = jnp.where(left, block, 0.0)[:40]
            wff[pl.ds(at + 38, 40), :] = jnp.where(left, pltpu.roll(block, 64, axis=1), 0.0)[:40]
    whole = wff[pl.ds(0, 2432), :].astype(BF16)

    arrived(tpr, rt)

    @pl.when(j > 0)
    def _():
        arrived(halo.at[0], rup)

    @pl.when(j < 15)
    def _():
        arrived(halo.at[1], rdn)

    for r in range(4):
        value = tp[r + 1] + tpr[r]
        if r == 0:
            value += halo[0, 0] + halo[0, 1]
        if r == 3:
            value += halo[1, 0] + halo[1, 1]
        gtd[pl.ds(r * 32, 32), :] = value.astype(BF16)

    prod = jnp.dot(nt2[...], gtd[...], preferred_element_type=F32).reshape(32, 48, 128)
    for k in range(16):
        nch[k] = jnp.where(left, prod[2 * k], prod[2 * k + 1]).astype(BF16)
    for step in range(1, 16):
        there = (j + step) % 16
        send(nch.at[there], nrb.at[j], rn, (mem, there * 2 + core))
    nrb[j] = nch[j]

    own_rows = pl.ds(pl.multiple_of(core * 64, 64), 64)
    gmod = lax.dot_general(gtd[own_rows, :], whole, (((1,), (1,)), ((), ())), preferred_element_type=F32)
    normed = nrm[own_rows, :]
    dn = gmod * (1.0 + scale)
    m1 = jnp.mean(dn, axis=-1, keepdims=True)
    m2 = jnp.mean(dn * normed, axis=-1, keepdims=True)
    gh_ref[0] = ((dn - m1 - normed * m2) * inv[own_rows, 0:1]).astype(BF16)

    arrived(nrb.at[pl.ds(0, 15)], rn)
    member = jnp.sum(nrb[...].astype(F32), axis=0)

    tokens_sum = member[38:39, :]
    weighted = own_scale * member + own_shift * tokens_sum
    for t in range(5):
        cm[t] = weighted[8 * t : 8 * t + 8]
        target = (OWNERS[t], sp)
        send(cm.at[t], mrb.at[mem], rm1, target, mem != OWNERS[t])

        @pl.when(mem == OWNERS[t])
        def _():
            mrb[mem] = cm[t]

    scaled = member * wide
    square = jnp.concatenate([scaled, jnp.zeros((80, 128), F32)], axis=0).T
    a = jnp.sum(square[:64], axis=0, keepdims=True)
    b = jnp.sum(square[64:], axis=0, keepdims=True)
    gsp[...] = jnp.concatenate([a, b, jnp.zeros((6, 128), F32)], axis=0)
    for step in range(1, 32):
        send(gsp, gsb.at[sp], rgs, (mem, (sp + step) % 32))
    gsb[sp] = gsp[...]

    high = tokens_sum.astype(BF16)
    low = (tokens_sum - high.astype(F32)).astype(BF16)
    pair = jnp.concatenate([high, low, jnp.zeros((14, 128), BF16)], axis=0)
    sums = lax.dot_general(pair, whole, (((1,), (1,)), ((), ())), preferred_element_type=F32)
    gsh_ref[...] = sums[0:1] + sums[1:2]

    for t in range(5):
        @pl.when(mem == OWNERS[t])
        def _():
            arrived(mrb.at[pl.ds(0, 15)], rm1)
            mab[t] = jnp.sum(mrb[...], axis=0)

        for step in range(1, 16):
            send(mab.at[t], mab.at[t], rm2.at[t], ((OWNERS[t] + step) % 16, sp), mem == OWNERS[t])

    arrived(gsb.at[pl.ds(0, 31)], rgs)
    for s in range(32):
        for h in range(2):
            gs_ref[:, pl.ds(76 * s + 38 * h, 38)] = gsb[s, h : h + 1, 0:38]

    for t in range(5):
        @pl.when(mem != OWNERS[t])
        def _():
            arrived(mab.at[t], rm2.at[t])
    final = mab[...].reshape(40, 128)
    gf_ref[pl.ds(0, 38), :] = final[:38, :64]
    gf_ref[pl.ds(38, 38), :] = final[:38, 64:]

    for copy, cond in pending:
        if cond is None:
            copy.wait_send()
        else:
            pl.when(cond)(copy.wait_send)


def per_device(grad_image, conv_weight, input_weight, hidden, shift, scale, final_weight):
    vmem = pl.BlockSpec(memory_space=pltpu.VMEM)
    hbm = pl.BlockSpec(memory_space=pl.ANY)
    dma = pltpu.SemaphoreType.DMA
    return pl.pallas_call(
        kernel,
        out_shape=(
            jax.ShapeDtypeStruct((1, 64, 2432), BF16),
            jax.ShapeDtypeStruct((76, 64), F32),
            jax.ShapeDtypeStruct((1, 2432), F32),
            jax.ShapeDtypeStruct((1, 2432), F32),
        ),
        in_specs=[hbm, vmem, vmem, hbm, vmem, vmem, vmem],
        out_specs=(vmem,) * 4,
        scratch_shapes=[
            pltpu.VMEM((16, 128, 256), BF16),
            pltpu.VMEM((2, 64, 2432), BF16),
            pltpu.VMEM((16, 16, 128), BF16),
            pltpu.VMEM((8, 16, 128), BF16),
            pltpu.VMEM((32, 16, 128), BF16),
            pltpu.VMEM((32, 16, 128), BF16),
            pltpu.VMEM((16, 8, 16, 128), BF16),
            pltpu.VMEM((8, 8, 16, 128), BF16),
            pltpu.VMEM((640, 2304), BF16),
            pltpu.VMEM((2, 144, 128), F32),
            pltpu.VMEM((2304, 256), BF16),
            pltpu.VMEM((640, 256), F32),
            pltpu.VMEM((768, 128), F32),
            pltpu.VMEM((6, 32, 128), F32),
            pltpu.VMEM((4, 32, 128), F32),
            pltpu.VMEM((2, 2, 32, 128), F32),
            pltpu.VMEM((2, 4, 4, 48, 128), BF16),
            pltpu.VMEM((2440, 128), F32),
            pltpu.VMEM((128, 2432), F32),
            pltpu.VMEM((128, 128), F32),
            pltpu.VMEM((2448, 128), F32),
            pltpu.VMEM((1536, 128), BF16),
            pltpu.VMEM((128, 128), BF16),
            pltpu.VMEM((16, 48, 128), BF16),
            pltpu.VMEM((16, 48, 128), BF16),
            pltpu.VMEM((8, 128), F32),
            pltpu.VMEM((32, 8, 128), F32),
            pltpu.VMEM((5, 8, 128), F32),
            pltpu.VMEM((16, 8, 128), F32),
            pltpu.VMEM((5, 8, 128), F32),
            dma((220,)),
            dma((2,)),
            dma, dma,
            dma, dma,
            dma((4,)), dma((2,)),
            dma, dma,
            dma, dma,
            dma((4,)), dma((4,)), dma,
            dma, dma, dma,
            dma, dma, dma, dma((5,)),
        ],
        compiler_params=pltpu.CompilerParams(
            collective_id=0, has_side_effects=True, vmem_limit_bytes=48 * 1024 * 1024
        ),
        cost_estimate=pl.CostEstimate(flops=1_000_000_000, bytes_accessed=2_000_000, transcendentals=0),
    )(
        grad_image,
        conv_weight.reshape(9, 16, 32),
        input_weight.reshape(144, 16),
        hidden,
        shift,
        scale,
        final_weight,
    )


def solution(mesh):
    placed = (
        P("mem", "sp", None, None),
        P(None, None, "sp", "mem"),
        P(None, None, None, "sp"),
        P("mem", "sp", None),
        P("mem", None),
        P("mem", None),
        P("sp", None),
    )
    return jax.shard_map(
        per_device,
        mesh=mesh,
        in_specs=placed,
        out_specs=(P("mem", "sp", None), P("sp", None), P("mem", None), P("mem", None)),
        check_vma=False,
    )
```

```python
import jax
import jax.numpy as jnp
from jax import lax
from jax.experimental import pallas as pl
from jax.experimental.pallas import tpu as pltpu
from jax.sharding import PartitionSpec as P

MESH = pl.DeviceIdType.MESH
F32, BF16 = jnp.float32, jnp.bfloat16
SPLIT = 10


def iota(shape, dim):
    return lax.broadcasted_iota(jnp.int32, shape, dim)


def kernel(
    g_hbm, cw_hbm, iw_hbm, hid_hbm, shift_hbm, scale_hbm, wf_hbm,
    gh_ref, gf_ref, gs_ref, gsh_ref,
    cwv, iwv, shv, scv, wfv,
    gall, hall, gother, pk, raw, kb, sx, ps, rhs, zacc, lat, tp, tpr, edge, halo,
    wfb, wff, whole, nrm, inv, ntf, nt2, gtd, nch, nrb, gmod, ghv, gst, cmb, mrb,
    ssem, lsem, rraw, rz, rzb, ry, ryb, rg, rh, rhu, rhd, rwy, rwx, rwc, rt, rn, rgc, rm,
):
    mem, sp = lax.axis_index("mem"), lax.axis_index("sp")
    ylo, z = mem // 8, mem % 8
    core, j = sp % 2, sp // 2
    yhi, x = j // 4, j % 4
    other = 1 - core
    pending = []
    used = [0]

    def send(src, dst, recv, device, cond=None):
        copy = pltpu.make_async_remote_copy(
            src_ref=src, dst_ref=dst, send_sem=ssem.at[used[0]], recv_sem=recv,
            device_id=device, device_id_type=MESH,
        )
        used[0] += 1
        pending.append((copy, cond))
        if cond is None:
            copy.start()
        else:
            pl.when(cond)(copy.start)

    def flush():
        for copy, cond in pending:
            if cond is None:
                copy.wait_send()
            else:
                pl.when(cond)(copy.wait_send)
        pending.clear()

    def arrived(ref, sem):
        pltpu.make_async_copy(ref, ref, sem).wait()

    barrier = pltpu.get_barrier_semaphore()

    def greet(device, cond=None):
        def signal():
            pl.semaphore_signal(barrier, inc=1, device_id=device, device_id_type=MESH)

        if cond is None:
            signal()
        else:
            pl.when(cond)(signal)

    def greet_sp(step, carry):
        greet((mem, (sp + step) % 32))
        return carry

    def greet_mem(step, carry):
        greet(((mem + step) % 16, sp))
        return carry

    lax.fori_loop(1, 32, greet_sp, 0)
    lax.fori_loop(1, 16, greet_mem, 0)

    loads = [
        (cw_hbm, cwv), (iw_hbm, iwv), (wf_hbm, wfv), (shift_hbm, shv), (scale_hbm, scv),
        (g_hbm.at[0, :, :, pl.ds(pl.multiple_of(core * 256, 256), 256)], gall.at[pl.ds(core * 8, 8)]),
        (hid_hbm.at[0], hall.at[core]),
        (g_hbm.at[0, :, :, pl.ds(pl.multiple_of(other * 256, 256), 256)], gother),
    ]
    loads = [pltpu.make_async_copy(src, dst, lsem.at[k]) for k, (src, dst) in enumerate(loads)]
    for copy in loads:
        copy.start()

    loads[0].wait()
    loads[1].wait()
    taps = iwv[...].astype(F32).T.astype(BF16)
    pk[...] = jnp.concatenate(
        [taps[:, :128]] + [cwv[k] for k in range(9)] + [taps[:, 128:], jnp.zeros((16, 80), BF16)], axis=1)

    loads[2].wait()
    wf = jnp.concatenate([wfv[...].astype(F32), jnp.zeros((64, 52), F32)], axis=1).T
    wide = jnp.concatenate([wf[:38], wf[38:76]], axis=1)
    wide = jnp.concatenate([wide, jnp.zeros((10, 128), F32)], axis=0)
    wfb[core, yhi, x] = wide.astype(BF16)

    pl.semaphore_wait(barrier, 46)

    source = core == ylo
    for step in range(16):
        target = (mem, ((j + step) % 16) * 2 + ylo)
        if step:
            send(pk, raw.at[sp], rraw, target)
        else:
            send(pk, raw.at[sp], rraw, target, jnp.logical_not(source))

    @pl.when(source)
    def _():
        pltpu.make_async_copy(pk, raw.at[sp], rraw).start()

    for step in range(1, 4):
        send(wfb.at[core, yhi, x], wfb.at[core, yhi, x], rwy.at[yhi], (mem, (((yhi + step) % 4) * 4 + x) * 2 + core))

    partner = (mem, j * 2 + other)
    loads[6].wait()
    send(hall.at[core], hall.at[core], rh, partner)
    loads[7].wait()
    send(gother, gall.at[pl.ds(core * 8, 8)], rg, partner)

    loads[3].wait()
    loads[4].wait()
    lanes = iota((48, 2432), 1)
    rows = iota((48, 2432), 0)
    hit_a, hit_b = lanes == sp * 76 + rows, lanes == sp * 76 + 38 + rows
    left = iota((48, 128), 1) < 64
    scale, shift = scv[...], shv[...]

    def pick(values):
        a = jnp.sum(jnp.where(hit_a, values, 0.0), axis=1, keepdims=True)
        b = jnp.sum(jnp.where(hit_b, values, 0.0), axis=1, keepdims=True)
        return jnp.where(left, a, b)

    own_scale, own_shift = 1.0 + pick(scale), pick(shift)

    arrived(hall.at[0], rh)
    for k in range(2):
        values = hall[k].astype(F32)
        centred = values - jnp.mean(values, axis=-1, keepdims=True)
        inverse = lax.rsqrt(jnp.mean(centred * centred, axis=-1, keepdims=True) + 1e-06)
        nrm[pl.ds(k * 64, 64), :] = centred * inverse
        inv[pl.ds(k * 64, 64), :] = jnp.broadcast_to(inverse, (64, 128))
    for k in range(19):
        ntf[pl.ds(k * 128, 128), :] = nrm[:, pl.ds(k * 128, 128)].T
    ntf[pl.ds(2432, 16), :] = jnp.zeros((16, 128), F32)
    row = iota((48, 128), 0)
    for k in range(16):
        for h in range(2):
            a = ntf[pl.ds(152 * k + 38 * h, 48), :]
            b = ntf[pl.ds(152 * k + 76 + 38 * h, 48), :]
            v = jnp.where(core == 0, a, b)
            v = jnp.where(row < 38, v, jnp.where(row == 38, 1.0, 0.0))
            nt2[pl.ds((2 * k + h) * 48, 48), :] = v.astype(BF16)

    loads[5].wait()
    arrived(gall.at[pl.ds(0, 8)], rg)

    for half in range(2):
        ps[half, pl.ds(0, 8), :] = jnp.zeros((8, 128), F32)
        ps[half, pl.ds(136, 8), :] = jnp.zeros((8, 128), F32)

    def columns(start):
        return jnp.concatenate([ps.at[half][pl.ds(start, 64, stride=2), :] for half in range(2)], axis=1)

    sx[pl.ds(0, 64), pl.ds(768, 1536)] = jnp.zeros((64, 1536), BF16)
    sx[pl.ds(576, 64), pl.ds(0, 1536)] = jnp.zeros((64, 1536), BF16)
    for r in range(-1, 16):
        pair = gall[max(r, 0)].astype(F32)
        if 0 <= r < 15:
            pair += gall[r + 1].astype(F32)
        for half in range(2):
            ps[half, pl.ds(8, 128), :] = pair[:, 128 * half : 128 * half + 128]
        before, even, odd, after = columns(7), columns(8), columns(9), columns(10)
        sums = jnp.concatenate([odd + after, even + odd, before + even], axis=1)
        if r % 2 == 0:
            places = ((r // 2, 1),)
        else:
            places = (((r - 1) // 2, 0), ((r + 1) // 2, 2))
        for i, a in places:
            kept = sums
            if i == -1:
                kept = jnp.where(j > 0, sums, 0.0)
            if i == 8:
                kept = jnp.where(j < 15, sums, 0.0)
            sx[pl.ds((i + 1) * 64, 64), pl.ds(a * 768, 768)] = kept.astype(BF16)

    for piece in range(4):
        @pl.when(yhi != piece)
        def _():
            arrived(wfb.at[core, piece, x], rwy.at[piece])
    for step in range(1, 4):
        send(wfb.at[core, :, x], wfb.at[core, :, x], rwx.at[x], (mem, (yhi * 4 + (x + step) % 4) * 2 + core))

    lane16 = iota((16, 128), 1) // 16

    @pl.when(source)
    def _():
        arrived(raw, rraw)
        every = raw[...].reshape(512, 512)
        ends = jnp.concatenate([every[:, :128], every[:, 384:]], axis=1)
        part = lax.dot_general(every[:, 128:], ends, (((0,), (0,)), ((), ())), preferred_element_type=F32)
        for k in range(18):
            kb[z, k] = part[16 * k : 16 * k + 16, :128].astype(BF16)
        for first in range(0, 24, 8):
            packed = jnp.zeros((16, 128), F32)
            for k in range(first, min(first + 8, 18)):
                moved = pltpu.roll(part[16 * k : 16 * k + 16, 128:], (16 * (k - first) - 32) % 128, axis=1)
                packed = jnp.where(lane16 == k - first, moved, packed)
            kb[z, 18 + first // 8] = packed.astype(BF16)

    across = ((1 - ylo) * 8 + z, sp)
    order = (1, 7, 2, 6, 3, 5, 4)
    sink = jnp.logical_not(source)
    one, two = pl.ds(0, SPLIT), pl.ds(SPLIT, 21 - SPLIT)

    send(kb.at[z, two], kb.at[z, two], ryb, across, source)
    for d in order:
        send(kb.at[z, one], kb.at[z, one], rz.at[z], (ylo * 8 + (z + d) % 8, sp), source)
    send(kb.at[z, one], kb.at[z, one], ry, across, source)

    @pl.when(sink)
    def _():
        arrived(kb.at[z, two], ryb)

    for d in order:
        send(kb.at[z, two], kb.at[z, two], rzb, (ylo * 8 + (z + d) % 8, sp))

    def forward(steps):
        for d in steps:
            there = (z + d) % 8

            @pl.when(source)
            def _():
                arrived(kb.at[there, one], rz.at[there])

            send(kb.at[there, one], kb.at[there, one], ry, across, source)

    forward(order[:4])

    for piece in range(4):
        @pl.when(x != piece)
        def _():
            arrived(wfb.at[core, :, piece], rwx.at[piece])
    send(wfb.at[core], wfb.at[core], rwc, partner)

    forward(order[4:])

    @pl.when(sink)
    def _():
        arrived(kb.at[:, one], ry)

    arrived(kb.at[pl.ds(0, 7), two], rzb)

    group = iota((8, 16, 128), 2) // 16
    for k in range(9):
        main, last = [], []
        for h in range(2):
            t = 2 * k + h
            main.append(kb[:, t])
            packed = kb[:, 18 + t // 8]
            last.append(jnp.where(group == t % 8, packed, jnp.zeros_like(packed)))
        pieces = []
        for zz in range(8):
            for h in range(2):
                pieces.append(jnp.concatenate([main[h][zz], last[h][zz]], axis=1))
        rhs[pl.ds(k * 256, 256), :] = jnp.concatenate(pieces, axis=0)

    zacc[...] = jnp.dot(sx[...], rhs[...], preferred_element_type=F32)

    field, corner = zacc[:, :128], zacc[:, 128:]
    column = iota((640, 128), 0) % 64
    g8 = iota((640, 128), 1) // 16
    tap_r, tap_c = g8 // 3, g8 % 3
    minus = jnp.where(column == 63, 0.0, pltpu.roll(field, 639, axis=0))
    plus = jnp.where(column == 0, 0.0, pltpu.roll(field, 1, axis=0))
    corner = jnp.where(column == 0, 0.0, pltpu.roll(corner, 1, axis=0))
    moved = jnp.where(tap_c == 0, minus, jnp.where(tap_c == 1, field, plus))
    none = jnp.zeros((64, 128), F32)
    total = jnp.concatenate([jnp.where(tap_r == 0, moved, 0.0), none, none], axis=0)
    total += jnp.concatenate([none, jnp.where(tap_r == 1, moved, 0.0), none], axis=0)
    total += jnp.concatenate([none, none, jnp.where(tap_r == 2, moved, 0.0) + corner], axis=0)
    total += pltpu.roll(total, 64, axis=1)
    total += pltpu.roll(total, 32, axis=1)
    total += pltpu.roll(total, 16, axis=1)
    lat[...] = total * (1.0 / 1.5305)
    g4 = (iota((32, 128), 1) // 16) % 4
    left16 = iota((16, 128), 1) < 64

    def unpack(packed):
        swapped = pltpu.roll(packed, 64, axis=1)
        return jnp.concatenate([jnp.where(left16, packed, swapped), jnp.where(left16, swapped, packed)], axis=0)

    for r in (0, 5, 1, 2, 3, 4):
        value = jnp.zeros((32, 128), F32)
        for p in range(2):
            for s in range(2):
                value = jnp.where(g4 == 2 * p + s, lat[pl.ds((2 * r + p) * 64 + s, 32, stride=2), :], value)
        if r == 0:
            edge[0] = jnp.where(left16, value[:16], value[16:])
        elif r == 5:
            edge[1] = jnp.where(left16, value[:16], value[16:])
            for c in range(2):
                send(edge.at[0], halo.at[1, core], rhd, (mem, jnp.maximum(2 * j - 2 + c, 0)), j > 0)
                send(edge.at[1], halo.at[0, core], rhu, (mem, jnp.minimum(2 * j + 2 + c, 31)), j < 15)
        else:
            tp[pl.ds((r - 1) * 32, 32), :] = value

    send(tp, tpr, rt, partner)

    @pl.when(j == 0)
    def _():
        halo[0] = jnp.zeros((2, 16, 128), F32)

    @pl.when(j == 15)
    def _():
        halo[1] = jnp.zeros((2, 16, 128), F32)

    arrived(wfb.at[0], rwc)
    for k in range(16):
        for c in range(2):
            block = wfb[c, k // 4, k % 4].astype(F32)
            at = 76 * (2 * k + c)
            wff[pl.ds(at, 40), :] = jnp.where(left, block, 0.0)[:40]
            wff[pl.ds(at + 38, 40), :] = jnp.where(left, pltpu.roll(block, 64, axis=1), 0.0)[:40]

    whole[...] = wff[pl.ds(0, 2432), :].astype(BF16)
    arrived(tpr, rt)

    @pl.when(j > 0)
    def _():
        arrived(halo.at[0], rhu)

    @pl.when(j < 15)
    def _():
        arrived(halo.at[1], rhd)

    above, below = unpack(halo[0, 0] + halo[0, 1]), unpack(halo[1, 0] + halo[1, 1])
    borders = jnp.concatenate([above, jnp.zeros((64, 128), F32), below], axis=0)
    gtd[...] = (tp[...] + tpr[...] + borders).astype(BF16)

    gmod[...] = lax.dot_general(gtd[...], whole[...], (((1,), (1,)), ((), ())), preferred_element_type=F32)
    line = jnp.sum(gmod[...] * nrm[...], axis=0, keepdims=True)
    low = [line[:, 128 * k : 128 * k + 128] for k in range(19)]
    low_rows = jnp.concatenate([pltpu.roll(low[9], 64, axis=1)] + low[:9], axis=0)
    high_rows = jnp.concatenate(low[9:], axis=0)
    shares = jnp.where(core == 0, low_rows, high_rows)

    prod = jnp.dot(nt2[...], gtd[...], preferred_element_type=F32).reshape(32, 48, 128)
    share = jnp.concatenate([jnp.zeros((38, 128), F32), shares], axis=0)
    spare = jnp.logical_or(row > 38, jnp.logical_and(row == 38, jnp.logical_not(left)))
    for k in range(16):
        nch[k] = jnp.where(spare, share, jnp.where(left, prod[2 * k], prod[2 * k + 1])).astype(BF16)
    for step in range(1, 16):
        there = (j + step) % 16
        send(nch.at[there], nrb.at[j], rn, (mem, there * 2 + core))
    nrb[j] = nch[j]

    mine = pl.ds(pl.multiple_of(core * 64, 64), 64)
    normed = nrm[mine, :]
    dn = gmod[mine, :] * (1.0 + scale)
    m1 = jnp.mean(dn, axis=-1, keepdims=True)
    m2 = jnp.mean(dn * normed, axis=-1, keepdims=True)
    ghv[...] = ((dn - m1 - normed * m2) * inv[mine, 0:1]).astype(BF16)
    out = pltpu.make_async_copy(ghv, gh_ref.at[0], lsem.at[0])
    out.start()
    flush()

    arrived(nrb.at[pl.ds(0, 15)], rn)
    member = jnp.sum(nrb[...].astype(F32), axis=0)

    tokens_sum = jnp.where(left[:1], member[38:39, :], pltpu.roll(member[38:39, :], 64, axis=1))
    cmb[...] = (own_scale * member + own_shift * tokens_sum).astype(BF16)
    for step in range(1, 16):
        send(cmb, mrb.at[mem], rm, ((mem + step) % 16, sp))
    mrb[mem] = cmb[...]

    gst[core] = jnp.concatenate([member[38:48], jnp.zeros((6, 128), F32)], axis=0)
    send(gst.at[core], gst.at[core], rgc, partner)
    high = tokens_sum.astype(BF16)
    low = (tokens_sum - high.astype(F32)).astype(BF16)
    pair = jnp.concatenate([high, low, jnp.zeros((14, 128), BF16)], axis=0)
    sums = lax.dot_general(pair, whole[...], (((1,), (1,)), ((), ())), preferred_element_type=F32)
    gsh_ref[...] = sums[0:1] + sums[1:2]

    flush()
    arrived(gst.at[0], rgc)
    middle = jnp.where(left[:1], pltpu.roll(gst[0, 0:1, :], 64, axis=1), gst[1, 0:1, :])
    gs_ref[...] = jnp.concatenate(
        [gst[0, k : k + 1, :] for k in range(1, 10)] + [middle] + [gst[1, k : k + 1, :] for k in range(1, 10)], axis=1)

    arrived(mrb.at[pl.ds(0, 15)], rm)
    final = jnp.sum(mrb[...].astype(F32), axis=0)
    square = jnp.concatenate([final, jnp.zeros((80, 128), F32)], axis=0).T
    lane = iota((64, 128), 1)
    out.wait()
    gf_ref[...] = jnp.where(lane < 38, square[:64], pltpu.roll(square[64:], 38, axis=1))[:, :76]


def place(*refs):
    ins, outs, held, sems = refs[:4], refs[4:8], refs[8:12], refs[12]
    reads = [pltpu.make_async_copy(ins[k], held[k], sems.at[k]) for k in range(4)]
    writes = [pltpu.make_async_copy(held[k], outs[k], sems.at[4 + k]) for k in range(4)]
    for copy in reads:
        copy.start()
    for k in (1, 2, 3, 0):
        reads[k].wait()
        writes[k].start()
    for copy in writes:
        copy.wait()


def per_device(grad_image, conv_weight, input_weight, hidden, shift, scale, final_weight):
    vmem = pl.BlockSpec(memory_space=pltpu.VMEM)
    hbm = pl.BlockSpec(memory_space=pl.ANY)
    dma = pltpu.SemaphoreType.DMA
    grad_hidden, grad_final, grad_scale, grad_shift = pl.pallas_call(
        kernel,
        out_shape=(
            jax.ShapeDtypeStruct((1, 64, 2432), BF16),
            jax.ShapeDtypeStruct((64, 76), F32),
            jax.ShapeDtypeStruct((1, 2432), F32),
            jax.ShapeDtypeStruct((1, 2432), F32),
        ),
        in_specs=[hbm] * 7,
        out_specs=(hbm, vmem, vmem, vmem),
        scratch_shapes=[
            pltpu.VMEM((9, 16, 32), BF16),
            pltpu.VMEM((144, 16), BF16),
            pltpu.VMEM((1, 2432), F32),
            pltpu.VMEM((1, 2432), F32),
            pltpu.VMEM((64, 76), BF16),
            pltpu.VMEM((16, 128, 256), BF16),
            pltpu.VMEM((2, 64, 2432), BF16),
            pltpu.VMEM((8, 128, 256), BF16),
            pltpu.VMEM((16, 512), BF16),
            pltpu.VMEM((32, 16, 512), BF16),
            pltpu.VMEM((8, 21, 16, 128), BF16),
            pltpu.VMEM((640, 2304), BF16),
            pltpu.VMEM((2, 144, 128), F32),
            pltpu.VMEM((2304, 256), BF16),
            pltpu.VMEM((640, 256), F32),
            pltpu.VMEM((768, 128), F32),
            pltpu.VMEM((128, 128), F32),
            pltpu.VMEM((128, 128), F32),
            pltpu.VMEM((2, 16, 128), F32),
            pltpu.VMEM((2, 2, 16, 128), F32),
            pltpu.VMEM((2, 4, 4, 48, 128), BF16),
            pltpu.VMEM((2440, 128), F32),
            pltpu.VMEM((2432, 128), BF16),
            pltpu.VMEM((128, 2432), F32),
            pltpu.VMEM((128, 128), F32),
            pltpu.VMEM((2448, 128), F32),
            pltpu.VMEM((1536, 128), BF16),
            pltpu.VMEM((128, 128), BF16),
            pltpu.VMEM((16, 48, 128), BF16),
            pltpu.VMEM((16, 48, 128), BF16),
            pltpu.VMEM((128, 2432), F32),
            pltpu.VMEM((64, 2432), BF16),
            pltpu.VMEM((2, 16, 128), F32),
            pltpu.VMEM((48, 128), BF16),
            pltpu.VMEM((16, 48, 128), BF16),
            dma((128,)),
            dma((8,)),
            dma, dma((8,)), dma, dma, dma,
            dma, dma, dma, dma,
            dma((4,)), dma((4,)), dma,
            dma, dma, dma, dma,
        ],
        compiler_params=pltpu.CompilerParams(
            collective_id=0, has_side_effects=True, vmem_limit_bytes=56 * 1024 * 1024
        ),
        cost_estimate=pl.CostEstimate(flops=1_000_000_000, bytes_accessed=2_000_000, transcendentals=0),
    )(
        grad_image,
        conv_weight.reshape(9, 16, 32),
        input_weight.reshape(144, 16),
        hidden,
        shift,
        scale,
        final_weight.T,
    )
    results = (grad_hidden, grad_final, grad_scale, grad_shift)
    grad_hidden, grad_final, grad_scale, grad_shift = pl.pallas_call(
        place,
        out_shape=tuple(jax.ShapeDtypeStruct(array.shape, array.dtype) for array in results),
        in_specs=[hbm] * 4,
        out_specs=(hbm,) * 4,
        scratch_shapes=[pltpu.VMEM(array.shape, array.dtype) for array in results] + [dma((8,))],
        compiler_params=pltpu.CompilerParams(vmem_limit_bytes=56 * 1024 * 1024),
    )(*results)
    return grad_hidden, grad_final.T, grad_scale, grad_shift


def solution(mesh):
    placed = (
        P("mem", "sp", None, None),
        P(None, None, "sp", "mem"),
        P(None, None, None, "sp"),
        P("mem", "sp", None),
        P("mem", None),
        P("mem", None),
        P("sp", None),
    )
    return jax.shard_map(
        per_device,
        mesh=mesh,
        in_specs=placed,
        out_specs=(P("mem", "sp", None), P("sp", None), P("mem", None), P("mem", None)),
        check_vma=False,
    )
```

```python
import jax
import jax.numpy as jnp
from jax import lax
from jax.experimental import pallas as pl
from jax.experimental.pallas import tpu as pltpu
from jax.sharding import PartitionSpec as P

MESH = pl.DeviceIdType.MESH
F32, BF16 = jnp.float32, jnp.bfloat16
SPLIT = 17


def iota(shape, dim):
    return lax.broadcasted_iota(jnp.int32, shape, dim)


def kernel(
    g_hbm, cw_hbm, iw_hbm, hid_hbm, shift_hbm, scale_hbm, wf_hbm,
    gh_ref, gf_ref, gs_ref, gsh_ref,
    cwv, iwv, shv, scv, wfv,
    gall, hall, gother, pk, raw, kb, sx, ps, rhs, zacc, lat, tp, tpr,
    wfb, wff, whole, nrm, inv, ntf, nt2, gtd, nch, nrb, gmod, ghv, gfv, gsv, gshv, gst, cmb, mrb,
    ssem, lsem, rraw, rz, rzb, ry, ryb, rg, rh, rhu, rhd, rwy, rwx, rwc, rt, rn, rgc, rm,
):
    mem, sp = lax.axis_index("mem"), lax.axis_index("sp")
    ylo, z = mem // 8, mem % 8
    core, j = sp % 2, sp // 2
    yhi, x = j // 4, j % 4
    other = 1 - core
    pending = []
    used = [0]

    def send(src, dst, recv, device, cond=None):
        copy = pltpu.make_async_remote_copy(
            src_ref=src, dst_ref=dst, send_sem=ssem.at[used[0]], recv_sem=recv,
            device_id=device, device_id_type=MESH,
        )
        used[0] += 1
        pending.append((copy, cond))
        if cond is None:
            copy.start()
        else:
            pl.when(cond)(copy.start)

    def flush():
        for copy, cond in pending:
            if cond is None:
                copy.wait_send()
            else:
                pl.when(cond)(copy.wait_send)
        pending.clear()

    def arrived(ref, sem):
        pltpu.make_async_copy(ref, ref, sem).wait()

    barrier = pltpu.get_barrier_semaphore()

    def greet(device, cond=None):
        def signal():
            pl.semaphore_signal(barrier, inc=1, device_id=device, device_id_type=MESH)

        if cond is None:
            signal()
        else:
            pl.when(cond)(signal)

    def greet_sp(step, carry):
        greet((mem, (sp + step) % 32))
        return carry

    def greet_mem(step, carry):
        greet(((mem + step) % 16, sp))
        return carry

    def beside(up):
        there = (2 * yhi + ylo + jnp.where(up, 1, 7)) % 8
        return ((there % 2) * 8 + z, ((there // 2) * 4 + x) * 2 + core)

    lax.fori_loop(1, 32, greet_sp, 0)
    lax.fori_loop(1, 16, greet_mem, 0)
    greet(beside(ylo == 1))

    loads = [
        (cw_hbm, cwv), (iw_hbm, iwv), (wf_hbm, wfv), (shift_hbm, shv), (scale_hbm, scv),
        (g_hbm.at[0, :, :, pl.ds(pl.multiple_of(core * 256, 256), 256)], gall.at[pl.ds(3 + core * 8, 8)]),
        (hid_hbm.at[0], hall.at[core]),
        (g_hbm.at[0, :, :, pl.ds(pl.multiple_of(other * 256, 256), 256)], gother),
    ]
    loads = [pltpu.make_async_copy(src, dst, lsem.at[k]) for k, (src, dst) in enumerate(loads)]
    for copy in loads:
        copy.start()

    loads[0].wait()
    loads[1].wait()
    taps = iwv[...].astype(F32).T.astype(BF16)
    pk[...] = jnp.concatenate(
        [taps[:, :128]] + [cwv[k] for k in range(9)] + [taps[:, 128:], jnp.zeros((16, 80), BF16)], axis=1)

    loads[2].wait()
    wf = jnp.concatenate([wfv[...].astype(F32), jnp.zeros((64, 52), F32)], axis=1).T
    wide = jnp.concatenate([wf[:38], wf[38:76]], axis=1)
    wide = jnp.concatenate([wide, jnp.zeros((10, 128), F32)], axis=0)
    wfb[core, yhi, x] = wide.astype(BF16)

    pl.semaphore_wait(barrier, 47)

    source = core == ylo
    for step in range(16):
        target = (mem, ((j + step) % 16) * 2 + ylo)
        if step:
            send(pk, raw.at[sp], rraw, target)
        else:
            send(pk, raw.at[sp], rraw, target, jnp.logical_not(source))

    @pl.when(source)
    def _():
        pltpu.make_async_copy(pk, raw.at[sp], rraw).start()

    for step in range(1, 4):
        send(wfb.at[core, yhi, x], wfb.at[core, yhi, x], rwy.at[yhi], (mem, (((yhi + step) % 4) * 4 + x) * 2 + core))

    partner = (mem, j * 2 + other)
    loads[6].wait()
    send(hall.at[core], hall.at[core], rh, partner)
    loads[7].wait()
    send(gother, gall.at[pl.ds(3 + core * 8, 8)], rg, partner)

    loads[3].wait()
    loads[4].wait()
    lanes = iota((48, 2432), 1)
    rows = iota((48, 2432), 0)
    hit_a, hit_b = lanes == sp * 76 + rows, lanes == sp * 76 + 38 + rows
    left = iota((48, 128), 1) < 64
    scale, shift = scv[...], shv[...]

    def pick(values):
        a = jnp.sum(jnp.where(hit_a, values, 0.0), axis=1, keepdims=True)
        b = jnp.sum(jnp.where(hit_b, values, 0.0), axis=1, keepdims=True)
        return jnp.where(left, a, b)

    own_scale, own_shift = 1.0 + pick(scale), pick(shift)

    arrived(hall.at[0], rh)
    for k in range(2):
        values = hall[k].astype(F32)
        centred = values - jnp.mean(values, axis=-1, keepdims=True)
        inverse = lax.rsqrt(jnp.mean(centred * centred, axis=-1, keepdims=True) + 1e-06)
        nrm[pl.ds(k * 64, 64), :] = centred * inverse
        inv[pl.ds(k * 64, 64), :] = jnp.broadcast_to(inverse, (64, 128))
    for k in range(19):
        ntf[pl.ds(k * 128, 128), :] = nrm[:, pl.ds(k * 128, 128)].T
    ntf[pl.ds(2432, 16), :] = jnp.zeros((16, 128), F32)
    row = iota((48, 128), 0)
    for k in range(16):
        for h in range(2):
            a = ntf[pl.ds(152 * k + 38 * h, 48), :]
            b = ntf[pl.ds(152 * k + 76 + 38 * h, 48), :]
            v = jnp.where(core == 0, a, b)
            v = jnp.where(row < 38, v, jnp.where(row == 38, 1.0, 0.0))
            nt2[pl.ds((2 * k + h) * 48, 48), :] = v.astype(BF16)

    loads[5].wait()
    arrived(gall.at[pl.ds(0, 8)], rg)

    for half in range(2):
        ps[half, pl.ds(0, 8), :] = jnp.zeros((8, 128), F32)
        ps[half, pl.ds(136, 8), :] = jnp.zeros((8, 128), F32)

    def columns(start):
        return jnp.concatenate([ps.at[half][pl.ds(start, 64, stride=2), :] for half in range(2)], axis=1)

    def windows(pairs):
        for r in pairs:
            pair = gall[r + 3].astype(F32) + gall[r + 4].astype(F32)
            for half in range(2):
                ps[half, pl.ds(8, 128), :] = pair[:, 128 * half : 128 * half + 128]
            before, even, odd, after = columns(7), columns(8), columns(9), columns(10)
            sums = jnp.concatenate([odd + after, even + odd, before + even], axis=1)
            if r % 2 == 0:
                places = ((r // 2, 1),)
            else:
                places = (((r - 1) // 2, 0), ((r + 1) // 2, 2))
            for i, a in places:
                if i < -1 or i > 8:
                    continue
                kept = sums
                if i == -1:
                    kept = jnp.where(j > 0, sums, 0.0)
                if i == 8:
                    kept = jnp.where(j < 15, sums, 0.0)
                sx[pl.ds((i + 1) * 64, 64), pl.ds(a * 768, 768)] = kept.astype(BF16)

    windows(range(0, 15))

    for piece in range(4):
        @pl.when(yhi != piece)
        def _():
            arrived(wfb.at[core, piece, x], rwy.at[piece])
    for step in range(1, 4):
        send(wfb.at[core, :, x], wfb.at[core, :, x], rwx.at[x], (mem, (yhi * 4 + (x + step) % 4) * 2 + core))

    lane16 = iota((16, 128), 1) // 16

    @pl.when(source)
    def _():
        arrived(raw, rraw)
        every = raw[...].reshape(512, 512)
        ends = jnp.concatenate([every[:, :128], every[:, 384:]], axis=1)
        part = lax.dot_general(every[:, 128:], ends, (((0,), (0,)), ((), ())), preferred_element_type=F32)
        for k in range(18):
            kb[z, k] = part[16 * k : 16 * k + 16, :128].astype(BF16)
        for first in range(0, 24, 8):
            packed = jnp.zeros((16, 128), F32)
            for k in range(first, min(first + 8, 18)):
                moved = pltpu.roll(part[16 * k : 16 * k + 16, 128:], (16 * (k - first) - 32) % 128, axis=1)
                packed = jnp.where(lane16 == k - first, moved, packed)
            kb[z, 18 + first // 8] = packed.astype(BF16)

    across = ((1 - ylo) * 8 + z, sp)
    order = (1, 7, 2, 6, 3, 5, 4)
    sink = jnp.logical_not(source)
    one, two = pl.ds(0, SPLIT), pl.ds(SPLIT, 21 - SPLIT)

    send(kb.at[z, two], kb.at[z, two], ryb, across, source)
    for d in order:
        send(kb.at[z, one], kb.at[z, one], rz.at[z], (ylo * 8 + (z + d) % 8, sp), source)
    send(kb.at[z, one], kb.at[z, one], ry, beside(z % 2 == 0), source)

    last, first = jnp.logical_and(core == 1, j < 15), jnp.logical_and(core == 0, j > 0)
    up, down = jnp.minimum(2 * j + 2, 30), jnp.maximum(2 * j - 2, 0)
    send(gall.at[pl.ds(16, 3)], gall.at[pl.ds(0, 3)], rhu, (mem, up + 1), last)
    send(gother.at[pl.ds(5, 3)], gall.at[pl.ds(0, 3)], rhu, (mem, up), last)
    send(gall.at[pl.ds(3, 3)], gall.at[pl.ds(19, 3)], rhd, (mem, down), first)
    send(gother.at[pl.ds(0, 3)], gall.at[pl.ds(19, 3)], rhd, (mem, down + 1), first)

    @pl.when(j == 0)
    def _():
        gall[pl.ds(0, 3)] = jnp.zeros((3, 128, 256), BF16)

    @pl.when(j == 15)
    def _():
        gall[pl.ds(19, 3)] = jnp.zeros((3, 128, 256), BF16)

    @pl.when(sink)
    def _():
        arrived(kb.at[z, two], ryb)

    for d in reversed(order):
        send(kb.at[z, two], kb.at[z, two], rzb, (ylo * 8 + (z + d) % 8, sp))

    def forward(steps):
        for d in steps:
            there = (z + d) % 8

            @pl.when(source)
            def _():
                arrived(kb.at[there, one], rz.at[there])

            send(kb.at[there, one], kb.at[there, one], ry, beside(there % 2 == 0), source)

    forward(order[:4])

    for piece in range(4):
        @pl.when(x != piece)
        def _():
            arrived(wfb.at[core, :, piece], rwx.at[piece])
    send(wfb.at[core], wfb.at[core], rwc, partner)

    forward(order[4:])

    @pl.when(j > 0)
    def _():
        arrived(gall.at[pl.ds(0, 3)], rhu)

    @pl.when(j < 15)
    def _():
        arrived(gall.at[pl.ds(0, 3)], rhd)

    windows((-3, -2, -1, 15, 16, 17))

    @pl.when(sink)
    def _():
        arrived(kb.at[:, one], ry)

    arrived(kb.at[pl.ds(0, 7), two], rzb)

    group = iota((8, 16, 128), 2) // 16
    for k in range(9):
        main, last = [], []
        for h in range(2):
            t = 2 * k + h
            main.append(kb[:, t])
            packed = kb[:, 18 + t // 8]
            last.append(jnp.where(group == t % 8, packed, jnp.zeros_like(packed)))
        pieces = []
        for zz in range(8):
            for h in range(2):
                pieces.append(jnp.concatenate([main[h][zz], last[h][zz]], axis=1))
        rhs[pl.ds(k * 256, 256), :] = jnp.concatenate(pieces, axis=0)

    zacc[...] = jnp.dot(sx[...], rhs[...], preferred_element_type=F32)

    field, corner = zacc[:, :128], zacc[:, 128:]
    column = iota((640, 128), 0) % 64
    g8 = iota((640, 128), 1) // 16
    tap_r, tap_c = g8 // 3, g8 % 3
    minus = jnp.where(column == 63, 0.0, pltpu.roll(field, 639, axis=0))
    plus = jnp.where(column == 0, 0.0, pltpu.roll(field, 1, axis=0))
    corner = jnp.where(column == 0, 0.0, pltpu.roll(corner, 1, axis=0))
    moved = jnp.where(tap_c == 0, minus, jnp.where(tap_c == 1, field, plus))
    row_r = tap_r[:512]
    total = jnp.where(row_r == 0, moved[128:], jnp.where(row_r == 1, moved[64:576], moved[:512])) + corner[:512]
    total += pltpu.roll(total, 64, axis=1)
    total += pltpu.roll(total, 32, axis=1)
    total += pltpu.roll(total, 16, axis=1)
    lat[...] = total * (1.0 / 1.5305)
    g4 = (iota((32, 128), 1) // 16) % 4
    for r in range(4):
        value = jnp.zeros((32, 128), F32)
        for p in range(2):
            for s in range(2):
                value = jnp.where(g4 == 2 * p + s, lat[pl.ds((2 * r + p) * 64 + s, 32, stride=2), :], value)
        tp[pl.ds(r * 32, 32), :] = value

    send(tp, tpr, rt, partner)

    arrived(wfb.at[0], rwc)
    for k in range(16):
        for c in range(2):
            block = wfb[c, k // 4, k % 4].astype(F32)
            at = 76 * (2 * k + c)
            wff[pl.ds(at, 40), :] = jnp.where(left, block, 0.0)[:40]
            wff[pl.ds(at + 38, 40), :] = jnp.where(left, pltpu.roll(block, 64, axis=1), 0.0)[:40]

    whole[...] = wff[pl.ds(0, 2432), :].astype(BF16)
    arrived(tpr, rt)
    gtd[...] = (tp[...] + tpr[...]).astype(BF16)

    gmod[...] = lax.dot_general(gtd[...], whole[...], (((1,), (1,)), ((), ())), preferred_element_type=F32)
    line = jnp.sum(gmod[...] * nrm[...], axis=0, keepdims=True)
    low = [line[:, 128 * k : 128 * k + 128] for k in range(19)]
    low_rows = jnp.concatenate([pltpu.roll(low[9], 64, axis=1)] + low[:9], axis=0)
    high_rows = jnp.concatenate(low[9:], axis=0)
    shares = jnp.where(core == 0, low_rows, high_rows)

    prod = jnp.dot(nt2[...], gtd[...], preferred_element_type=F32).reshape(32, 48, 128)
    share = jnp.concatenate([jnp.zeros((38, 128), F32), shares], axis=0)
    spare = jnp.logical_or(row > 38, jnp.logical_and(row == 38, jnp.logical_not(left)))
    for k in range(16):
        nch[k] = jnp.where(spare, share, jnp.where(left, prod[2 * k], prod[2 * k + 1])).astype(BF16)
    for step in range(1, 16):
        there = (j + step) % 16
        send(nch.at[there], nrb.at[j], rn, (mem, there * 2 + core))
    nrb[j] = nch[j]

    mine = pl.ds(pl.multiple_of(core * 64, 64), 64)
    normed = nrm[mine, :]
    dn = gmod[mine, :] * (1.0 + scale)
    m1 = jnp.mean(dn, axis=-1, keepdims=True)
    m2 = jnp.mean(dn * normed, axis=-1, keepdims=True)
    ghv[...] = ((dn - m1 - normed * m2) * inv[mine, 0:1]).astype(BF16)
    out = pltpu.make_async_copy(ghv, gh_ref.at[0], lsem.at[0])
    out.start()
    flush()

    arrived(nrb.at[pl.ds(0, 15)], rn)
    member = jnp.sum(nrb[...].astype(F32), axis=0)

    tokens_sum = jnp.where(left[:1], member[38:39, :], pltpu.roll(member[38:39, :], 64, axis=1))
    cmb[...] = (own_scale * member + own_shift * tokens_sum).astype(BF16)
    for step in range(1, 16):
        send(cmb, mrb.at[mem], rm, ((mem + step) % 16, sp))
    mrb[mem] = cmb[...]

    gst[core] = jnp.concatenate([member[38:48], jnp.zeros((6, 128), F32)], axis=0)
    send(gst.at[core], gst.at[core], rgc, partner)
    high = tokens_sum.astype(BF16)
    low = (tokens_sum - high.astype(F32)).astype(BF16)
    pair = jnp.concatenate([high, low, jnp.zeros((14, 128), BF16)], axis=0)
    sums = lax.dot_general(pair, whole[...], (((1,), (1,)), ((), ())), preferred_element_type=F32)
    gshv[...] = sums[0:1] + sums[1:2]
    out_gsh = pltpu.make_async_copy(gshv, gsh_ref, lsem.at[1])
    out_gsh.start()

    flush()
    arrived(gst.at[0], rgc)
    middle = jnp.where(left[:1], pltpu.roll(gst[0, 0:1, :], 64, axis=1), gst[1, 0:1, :])
    gsv[...] = jnp.concatenate(
        [gst[0, k : k + 1, :] for k in range(1, 10)] + [middle] + [gst[1, k : k + 1, :] for k in range(1, 10)], axis=1)

    out_gs = pltpu.make_async_copy(gsv, gs_ref, lsem.at[2])
    out_gs.start()
    arrived(mrb.at[pl.ds(0, 15)], rm)
    final = jnp.sum(mrb[...].astype(F32), axis=0)
    square = jnp.concatenate([final, jnp.zeros((80, 128), F32)], axis=0).T
    lane = iota((64, 128), 1)
    gfv[...] = jnp.where(lane < 38, square[:64], pltpu.roll(square[64:], 38, axis=1))[:, :76]
    out_gf = pltpu.make_async_copy(gfv, gf_ref, lsem.at[3])
    out_gf.start()
    flush()
    for copy in (out, out_gsh, out_gs, out_gf):
        copy.wait()


def place(*refs):
    ins, outs, held, sems = refs[:4], refs[4:8], refs[8:12], refs[12]
    reads = [pltpu.make_async_copy(ins[k], held[k], sems.at[k]) for k in range(4)]
    writes = [pltpu.make_async_copy(held[k], outs[k], sems.at[4 + k]) for k in range(4)]
    for copy in reads:
        copy.start()
    for k in (1, 2, 3, 0):
        reads[k].wait()
        writes[k].start()
    for copy in writes:
        copy.wait()


def per_device(grad_image, conv_weight, input_weight, hidden, shift, scale, final_weight):
    hbm = pl.BlockSpec(memory_space=pl.ANY)
    dma = pltpu.SemaphoreType.DMA
    grad_hidden, grad_final, grad_scale, grad_shift = pl.pallas_call(
        kernel,
        out_shape=(
            jax.ShapeDtypeStruct((1, 64, 2432), BF16),
            jax.ShapeDtypeStruct((64, 76), F32),
            jax.ShapeDtypeStruct((1, 2432), F32),
            jax.ShapeDtypeStruct((1, 2432), F32),
        ),
        in_specs=[hbm] * 7,
        out_specs=(hbm,) * 4,
        scratch_shapes=[
            pltpu.VMEM((9, 16, 32), BF16),
            pltpu.VMEM((144, 16), BF16),
            pltpu.VMEM((1, 2432), F32),
            pltpu.VMEM((1, 2432), F32),
            pltpu.VMEM((64, 76), BF16),
            pltpu.VMEM((22, 128, 256), BF16),
            pltpu.VMEM((2, 64, 2432), BF16),
            pltpu.VMEM((8, 128, 256), BF16),
            pltpu.VMEM((16, 512), BF16),
            pltpu.VMEM((32, 16, 512), BF16),
            pltpu.VMEM((8, 21, 16, 128), BF16),
            pltpu.VMEM((640, 2304), BF16),
            pltpu.VMEM((2, 144, 128), F32),
            pltpu.VMEM((2304, 256), BF16),
            pltpu.VMEM((640, 256), F32),
            pltpu.VMEM((512, 128), F32),
            pltpu.VMEM((128, 128), F32),
            pltpu.VMEM((128, 128), F32),
            pltpu.VMEM((2, 4, 4, 48, 128), BF16),
            pltpu.VMEM((2440, 128), F32),
            pltpu.VMEM((2432, 128), BF16),
            pltpu.VMEM((128, 2432), F32),
            pltpu.VMEM((128, 128), F32),
            pltpu.VMEM((2448, 128), F32),
            pltpu.VMEM((1536, 128), BF16),
            pltpu.VMEM((128, 128), BF16),
            pltpu.VMEM((16, 48, 128), BF16),
            pltpu.VMEM((16, 48, 128), BF16),
            pltpu.VMEM((128, 2432), F32),
            pltpu.VMEM((64, 2432), BF16),
            pltpu.VMEM((64, 76), F32),
            pltpu.VMEM((1, 2432), F32),
            pltpu.VMEM((1, 2432), F32),
            pltpu.VMEM((2, 16, 128), F32),
            pltpu.VMEM((48, 128), BF16),
            pltpu.VMEM((16, 48, 128), BF16),
            dma((128,)),
            dma((8,)),
            dma, dma((8,)), dma, dma, dma,
            dma, dma, dma, dma,
            dma((4,)), dma((4,)), dma,
            dma, dma, dma, dma,
        ],
        compiler_params=pltpu.CompilerParams(
            collective_id=0, has_side_effects=True, vmem_limit_bytes=56 * 1024 * 1024
        ),
        cost_estimate=pl.CostEstimate(flops=1_000_000_000, bytes_accessed=2_000_000, transcendentals=0),
    )(
        grad_image,
        conv_weight.reshape(9, 16, 32),
        input_weight.reshape(144, 16),
        hidden,
        shift,
        scale,
        final_weight.T,
    )
    results = (grad_hidden, grad_final, grad_scale, grad_shift)
    grad_hidden, grad_final, grad_scale, grad_shift = pl.pallas_call(
        place,
        out_shape=tuple(jax.ShapeDtypeStruct(array.shape, array.dtype) for array in results),
        in_specs=[hbm] * 4,
        out_specs=(hbm,) * 4,
        scratch_shapes=[pltpu.VMEM(array.shape, array.dtype) for array in results] + [dma((8,))],
        compiler_params=pltpu.CompilerParams(vmem_limit_bytes=56 * 1024 * 1024),
    )(*results)
    return grad_hidden, grad_final.T, grad_scale, grad_shift


def solution(mesh):
    placed = (
        P("mem", "sp", None, None),
        P(None, None, "sp", "mem"),
        P(None, None, None, "sp"),
        P("mem", "sp", None),
        P("mem", None),
        P("mem", None),
        P("sp", None),
    )
    return jax.shard_map(
        per_device,
        mesh=mesh,
        in_specs=placed,
        out_specs=(P("mem", "sp", None), P("sp", None), P("mem", None), P("mem", None)),
        check_vma=False,
    )
```

```python
import jax
import jax.numpy as jnp
from jax import lax
from jax.experimental import pallas as pl
from jax.experimental.pallas import tpu as pltpu
from jax.sharding import PartitionSpec as P

MESH = pl.DeviceIdType.MESH
F32, BF16 = jnp.float32, jnp.bfloat16
SPLIT = 17


def iota(shape, dim):
    return lax.broadcasted_iota(jnp.int32, shape, dim)


def kernel(
    g_hbm, cw_hbm, iw_hbm, hid_hbm, shift_hbm, scale_hbm, wf_hbm,
    gh_ref, gf_ref, gs_ref, gsh_ref,
    cwv, iwv, shv, scv, wfv,
    gall, hall, gother, pk, raw, kb, sx, ps, rhs, zacc, lat, tp, tpr,
    wfb, wff, whole, nrm, inv, ntf, nt2, gtd, nch, nrb, gmod, ghv, gfv, gsv, gshv, gst, cmb, mrb,
    ssem, lsem, rraw, rz, rzb, ry, ryb, rg, rh, rhu, rhd, rwy, rwx, rwc, rt, rn, rgc, rm,
):
    mem, sp = lax.axis_index("mem"), lax.axis_index("sp")
    ylo, z = mem // 8, mem % 8
    core, j = sp % 2, sp // 2
    yhi, x = j // 4, j % 4
    other = 1 - core
    pending = []
    used = [0]

    def send(src, dst, recv, device, cond=None):
        copy = pltpu.make_async_remote_copy(
            src_ref=src, dst_ref=dst, send_sem=ssem.at[used[0]], recv_sem=recv,
            device_id=device, device_id_type=MESH,
        )
        used[0] += 1
        pending.append((copy, cond))
        if cond is None:
            copy.start()
        else:
            pl.when(cond)(copy.start)

    def flush():
        for copy, cond in pending:
            if cond is None:
                copy.wait_send()
            else:
                pl.when(cond)(copy.wait_send)
        pending.clear()

    def arrived(ref, sem):
        pltpu.make_async_copy(ref, ref, sem).wait()

    barrier = pltpu.get_barrier_semaphore()

    def greet(device, cond=None):
        def signal():
            pl.semaphore_signal(barrier, inc=1, device_id=device, device_id_type=MESH)

        if cond is None:
            signal()
        else:
            pl.when(cond)(signal)

    def greet_sp(step, carry):
        greet((mem, (sp + step) % 32))
        return carry

    def greet_mem(step, carry):
        greet(((mem + step) % 16, sp))
        return carry

    def beside(up):
        there = (2 * yhi + ylo + jnp.where(up, 1, 7)) % 8
        return ((there % 2) * 8 + z, ((there // 2) * 4 + x) * 2 + core)

    lax.fori_loop(1, 32, greet_sp, 0)
    lax.fori_loop(1, 16, greet_mem, 0)
    greet(beside(ylo == 1))

    loads = [
        (cw_hbm, cwv), (iw_hbm, iwv), (wf_hbm, wfv), (shift_hbm, shv), (scale_hbm, scv),
        (g_hbm.at[0, :, :, pl.ds(pl.multiple_of(core * 256, 256), 256)], gall.at[pl.ds(3 + core * 8, 8)]),
        (hid_hbm.at[0], hall.at[core]),
        (g_hbm.at[0, :, :, pl.ds(pl.multiple_of(other * 256, 256), 256)], gother),
    ]
    loads = [pltpu.make_async_copy(src, dst, lsem.at[k]) for k, (src, dst) in enumerate(loads)]
    for copy in loads:
        copy.start()

    loads[0].wait()
    loads[1].wait()
    taps = iwv[...].astype(F32).T.astype(BF16)
    pk[...] = jnp.concatenate(
        [taps[:, :128]] + [cwv[k] for k in range(9)] + [taps[:, 128:], jnp.zeros((16, 80), BF16)], axis=1)

    loads[2].wait()
    wf = jnp.concatenate([wfv[...].astype(F32), jnp.zeros((64, 52), F32)], axis=1).T
    wide = jnp.concatenate([wf[:38], wf[38:76]], axis=1)
    wide = jnp.concatenate([wide, jnp.zeros((10, 128), F32)], axis=0)
    wfb[core, yhi, x] = wide.astype(BF16)

    pl.semaphore_wait(barrier, 47)

    source = core == ylo
    for step in range(16):
        target = (mem, ((j + step) % 16) * 2 + ylo)
        if step:
            send(pk, raw.at[sp], rraw, target)
        else:
            send(pk, raw.at[sp], rraw, target, jnp.logical_not(source))

    @pl.when(source)
    def _():
        pltpu.make_async_copy(pk, raw.at[sp], rraw).start()

    for step in range(1, 4):
        send(wfb.at[core, yhi, x], wfb.at[core, yhi, x], rwy.at[yhi], (mem, (((yhi + step) % 4) * 4 + x) * 2 + core))

    partner = (mem, j * 2 + other)
    loads[6].wait()
    send(hall.at[core], hall.at[core], rh, partner)
    loads[7].wait()
    send(gother, gall.at[pl.ds(3 + core * 8, 8)], rg, partner)

    loads[3].wait()
    loads[4].wait()
    lanes = iota((48, 2432), 1)
    rows = iota((48, 2432), 0)
    hit_a, hit_b = lanes == sp * 76 + rows, lanes == sp * 76 + 38 + rows
    left = iota((48, 128), 1) < 64
    scale, shift = scv[...], shv[...]

    def pick(values):
        a = jnp.sum(jnp.where(hit_a, values, 0.0), axis=1, keepdims=True)
        b = jnp.sum(jnp.where(hit_b, values, 0.0), axis=1, keepdims=True)
        return jnp.where(left, a, b)

    own_scale, own_shift = 1.0 + pick(scale), pick(shift)

    arrived(hall.at[0], rh)
    for k in range(2):
        values = hall[k].astype(F32)
        centred = values - jnp.mean(values, axis=-1, keepdims=True)
        inverse = lax.rsqrt(jnp.mean(centred * centred, axis=-1, keepdims=True) + 1e-06)
        nrm[pl.ds(k * 64, 64), :] = centred * inverse
        inv[pl.ds(k * 64, 64), :] = jnp.broadcast_to(inverse, (64, 128))
    for k in range(19):
        ntf[pl.ds(k * 128, 128), :] = nrm[:, pl.ds(k * 128, 128)].T
    ntf[pl.ds(2432, 16), :] = jnp.zeros((16, 128), F32)
    row = iota((48, 128), 0)
    for k in range(16):
        for h in range(2):
            a = ntf[pl.ds(152 * k + 38 * h, 48), :]
            b = ntf[pl.ds(152 * k + 76 + 38 * h, 48), :]
            v = jnp.where(core == 0, a, b)
            v = jnp.where(row < 38, v, jnp.where(row == 38, 1.0, 0.0))
            nt2[pl.ds((2 * k + h) * 48, 48), :] = v.astype(BF16)

    loads[5].wait()
    arrived(gall.at[pl.ds(0, 8)], rg)

    for half in range(2):
        ps[half, pl.ds(0, 8), :] = jnp.zeros((8, 128), F32)
        ps[half, pl.ds(136, 8), :] = jnp.zeros((8, 128), F32)

    def columns(start):
        return jnp.concatenate([ps.at[half][pl.ds(start, 64, stride=2), :] for half in range(2)], axis=1)

    def windows(pairs):
        for r in pairs:
            pair = gall[r + 3].astype(F32) + gall[r + 4].astype(F32)
            for half in range(2):
                ps[half, pl.ds(8, 128), :] = pair[:, 128 * half : 128 * half + 128]
            before, even, odd, after = columns(7), columns(8), columns(9), columns(10)
            sums = jnp.concatenate([odd + after, even + odd, before + even], axis=1)
            if r % 2 == 0:
                places = ((r // 2, 1),)
            else:
                places = (((r - 1) // 2, 0), ((r + 1) // 2, 2))
            for i, a in places:
                if i < -1 or i > 8:
                    continue
                kept = sums
                if i == -1:
                    kept = jnp.where(j > 0, sums, 0.0)
                if i == 8:
                    kept = jnp.where(j < 15, sums, 0.0)
                sx[pl.ds((i + 1) * 64, 64), pl.ds(a * 768, 768)] = kept.astype(BF16)

    windows(range(0, 15))

    for piece in range(4):
        @pl.when(yhi != piece)
        def _():
            arrived(wfb.at[core, piece, x], rwy.at[piece])
    for step in range(1, 4):
        send(wfb.at[core, :, x], wfb.at[core, :, x], rwx.at[x], (mem, (yhi * 4 + (x + step) % 4) * 2 + core))

    lane16 = iota((16, 128), 1) // 16

    @pl.when(source)
    def _():
        arrived(raw, rraw)
        every = raw[...].reshape(512, 512)
        ends = jnp.concatenate([every[:, :128], every[:, 384:]], axis=1)
        part = lax.dot_general(every[:, 128:], ends, (((0,), (0,)), ((), ())), preferred_element_type=F32)
        for k in range(18):
            kb[z, k] = part[16 * k : 16 * k + 16, :128].astype(BF16)
        for first in range(0, 24, 8):
            packed = jnp.zeros((16, 128), F32)
            for k in range(first, min(first + 8, 18)):
                moved = pltpu.roll(part[16 * k : 16 * k + 16, 128:], (16 * (k - first) - 32) % 128, axis=1)
                packed = jnp.where(lane16 == k - first, moved, packed)
            kb[z, 18 + first // 8] = packed.astype(BF16)

    across = ((1 - ylo) * 8 + z, sp)
    order = (1, 7, 2, 6, 3, 5, 4)
    sink = jnp.logical_not(source)
    one, two = pl.ds(0, SPLIT), pl.ds(SPLIT, 21 - SPLIT)

    send(kb.at[z, two], kb.at[z, two], ryb, across, source)
    for d in order:
        send(kb.at[z, one], kb.at[z, one], rz.at[z], (ylo * 8 + (z + d) % 8, sp), source)
    send(kb.at[z, one], kb.at[z, one], ry, beside(z % 2 == 0), source)

    last, first = jnp.logical_and(core == 1, j < 15), jnp.logical_and(core == 0, j > 0)
    up, down = jnp.minimum(2 * j + 2, 30), jnp.maximum(2 * j - 2, 0)
    send(gall.at[pl.ds(16, 3)], gall.at[pl.ds(0, 3)], rhu, (mem, up + 1), last)
    send(gother.at[pl.ds(5, 3)], gall.at[pl.ds(0, 3)], rhu, (mem, up), last)
    send(gall.at[pl.ds(3, 3)], gall.at[pl.ds(19, 3)], rhd, (mem, down), first)
    send(gother.at[pl.ds(0, 3)], gall.at[pl.ds(19, 3)], rhd, (mem, down + 1), first)

    @pl.when(j == 0)
    def _():
        gall[pl.ds(0, 3)] = jnp.zeros((3, 128, 256), BF16)

    @pl.when(j == 15)
    def _():
        gall[pl.ds(19, 3)] = jnp.zeros((3, 128, 256), BF16)

    @pl.when(sink)
    def _():
        arrived(kb.at[z, two], ryb)

    for d in reversed(order):
        send(kb.at[z, two], kb.at[z, two], rzb, (ylo * 8 + (z + d) % 8, sp))

    def forward(steps):
        for d in steps:
            there = (z + d) % 8

            @pl.when(source)
            def _():
                arrived(kb.at[there, one], rz.at[there])

            send(kb.at[there, one], kb.at[there, one], ry, beside(there % 2 == 0), source)

    forward(order[:4])

    for piece in range(4):
        @pl.when(x != piece)
        def _():
            arrived(wfb.at[core, :, piece], rwx.at[piece])
    send(wfb.at[core], wfb.at[core], rwc, partner)

    forward(order[4:])

    @pl.when(j > 0)
    def _():
        arrived(gall.at[pl.ds(0, 3)], rhu)

    @pl.when(j < 15)
    def _():
        arrived(gall.at[pl.ds(0, 3)], rhd)

    windows((-3, -2, -1, 15, 16, 17))

    @pl.when(sink)
    def _():
        arrived(kb.at[:, one], ry)

    arrived(kb.at[pl.ds(0, 7), two], rzb)

    group = iota((8, 16, 128), 2) // 16
    for k in range(9):
        main, last = [], []
        for h in range(2):
            t = 2 * k + h
            main.append(kb[:, t])
            packed = kb[:, 18 + t // 8]
            last.append(jnp.where(group == t % 8, packed, jnp.zeros_like(packed)))
        pieces = []
        for zz in range(8):
            for h in range(2):
                pieces.append(jnp.concatenate([main[h][zz], last[h][zz]], axis=1))
        rhs[pl.ds(k * 256, 256), :] = jnp.concatenate(pieces, axis=0)

    zacc[...] = jnp.dot(sx[...], rhs[...], preferred_element_type=F32)

    field, corner = zacc[:, :128], zacc[:, 128:]
    column = iota((640, 128), 0) % 64
    g8 = iota((640, 128), 1) // 16
    tap_r, tap_c = g8 // 3, g8 % 3
    minus = jnp.where(column == 63, 0.0, pltpu.roll(field, 639, axis=0))
    plus = jnp.where(column == 0, 0.0, pltpu.roll(field, 1, axis=0))
    corner = jnp.where(column == 0, 0.0, pltpu.roll(corner, 1, axis=0))
    moved = jnp.where(tap_c == 0, minus, jnp.where(tap_c == 1, field, plus))
    row_r = tap_r[:512]
    total = jnp.where(row_r == 0, moved[128:], jnp.where(row_r == 1, moved[64:576], moved[:512])) + corner[:512]
    total += pltpu.roll(total, 64, axis=1)
    total += pltpu.roll(total, 32, axis=1)
    total += pltpu.roll(total, 16, axis=1)
    lat[...] = total * (1.0 / 1.5305)
    g4 = (iota((32, 128), 1) // 16) % 4
    for r in range(4):
        value = jnp.zeros((32, 128), F32)
        for p in range(2):
            for s in range(2):
                value = jnp.where(g4 == 2 * p + s, lat[pl.ds((2 * r + p) * 64 + s, 32, stride=2), :], value)
        tp[pl.ds(r * 32, 32), :] = value

    send(tp, tpr, rt, partner)

    arrived(wfb.at[0], rwc)
    for k in range(16):
        for c in range(2):
            block = wfb[c, k // 4, k % 4].astype(F32)
            at = 76 * (2 * k + c)
            wff[pl.ds(at, 40), :] = jnp.where(left, block, 0.0)[:40]
            wff[pl.ds(at + 38, 40), :] = jnp.where(left, pltpu.roll(block, 64, axis=1), 0.0)[:40]

    whole[...] = wff[pl.ds(0, 2432), :].astype(BF16)
    arrived(tpr, rt)
    gtd[...] = (tp[...] + tpr[...]).astype(BF16)

    gmod[...] = lax.dot_general(gtd[...], whole[...], (((1,), (1,)), ((), ())), preferred_element_type=F32)
    line = jnp.sum(gmod[...] * nrm[...], axis=0, keepdims=True)
    low = [line[:, 128 * k : 128 * k + 128] for k in range(19)]
    low_rows = jnp.concatenate([pltpu.roll(low[9], 64, axis=1)] + low[:9], axis=0)
    high_rows = jnp.concatenate(low[9:], axis=0)
    shares = jnp.where(core == 0, low_rows, high_rows)

    prod = jnp.dot(nt2[...], gtd[...], preferred_element_type=F32).reshape(32, 48, 128)
    share = jnp.concatenate([jnp.zeros((38, 128), F32), shares], axis=0)
    spare = jnp.logical_or(row > 38, jnp.logical_and(row == 38, jnp.logical_not(left)))
    for k in range(16):
        nch[k] = jnp.where(spare, share, jnp.where(left, prod[2 * k], prod[2 * k + 1])).astype(BF16)
    for step in range(1, 16):
        there = (j + step) % 16
        send(nch.at[there], nrb.at[j], rn, (mem, there * 2 + core))
    nrb[j] = nch[j]

    mine = pl.ds(pl.multiple_of(core * 64, 64), 64)
    normed = nrm[mine, :]
    dn = gmod[mine, :] * (1.0 + scale)
    m1 = jnp.mean(dn, axis=-1, keepdims=True)
    m2 = jnp.mean(dn * normed, axis=-1, keepdims=True)
    ghv[...] = ((dn - m1 - normed * m2) * inv[mine, 0:1]).astype(BF16)
    out = pltpu.make_async_copy(ghv, gh_ref.at[0], lsem.at[0])
    out.start()
    flush()

    arrived(nrb.at[pl.ds(0, 15)], rn)
    member = jnp.sum(nrb[...].astype(F32), axis=0)

    tokens_sum = jnp.where(left[:1], member[38:39, :], pltpu.roll(member[38:39, :], 64, axis=1))
    cmb[...] = (own_scale * member + own_shift * tokens_sum).astype(BF16)
    for step in range(1, 16):
        send(cmb, mrb.at[mem], rm, ((mem + step) % 16, sp))
    mrb[mem] = cmb[...]

    gst[core] = jnp.concatenate([member[38:48], jnp.zeros((6, 128), F32)], axis=0)
    send(gst.at[core], gst.at[core], rgc, partner)
    high = tokens_sum.astype(BF16)
    low = (tokens_sum - high.astype(F32)).astype(BF16)
    pair = jnp.concatenate([high, low, jnp.zeros((14, 128), BF16)], axis=0)
    sums = lax.dot_general(pair, whole[...], (((1,), (1,)), ((), ())), preferred_element_type=F32)
    gshv[...] = sums[0:1] + sums[1:2]
    out_gsh = pltpu.make_async_copy(gshv, gsh_ref, lsem.at[1])
    out_gsh.start()

    flush()
    arrived(gst.at[0], rgc)
    middle = jnp.where(left[:1], pltpu.roll(gst[0, 0:1, :], 64, axis=1), gst[1, 0:1, :])
    gsv[...] = jnp.concatenate(
        [gst[0, k : k + 1, :] for k in range(1, 10)] + [middle] + [gst[1, k : k + 1, :] for k in range(1, 10)], axis=1)

    out_gs = pltpu.make_async_copy(gsv, gs_ref, lsem.at[2])
    out_gs.start()
    arrived(mrb.at[pl.ds(0, 15)], rm)
    final = jnp.sum(mrb[...].astype(F32), axis=0)
    square = jnp.concatenate([final, jnp.zeros((80, 128), F32)], axis=0).T
    lane = iota((64, 128), 1)
    gfv[...] = jnp.where(lane < 38, square[:64], pltpu.roll(square[64:], 38, axis=1))[:, :76]
    out_gf = pltpu.make_async_copy(gfv, gf_ref, lsem.at[3])
    out_gf.start()
    flush()
    for copy in (out, out_gsh, out_gs, out_gf):
        copy.wait()


def place(*refs):
    ins, outs, held, sems = refs[:4], refs[4:8], refs[8:12], refs[12]
    views = [lambda ref: ref] * 3 + [lambda ref, k=k: ref.at[0, pl.ds(16 * k, 16)] for k in range(4)]
    which = (1, 2, 3, 0, 0, 0, 0)
    reads, writes = [], []
    for n, (view, k) in enumerate(zip(views, which)):
        reads.append(pltpu.make_async_copy(view(ins[k]), view(held[k]), sems.at[n]))
        writes.append(pltpu.make_async_copy(view(held[k]), view(outs[k]), sems.at[7 + n]))
    for n in (3, 4, 5, 6, 0, 1, 2):
        reads[n].start()
    for n in (3, 4, 5, 6, 0, 1, 2):
        reads[n].wait()
        writes[n].start()
    for copy in writes:
        copy.wait()


def per_device(grad_image, conv_weight, input_weight, hidden, shift, scale, final_weight):
    hbm = pl.BlockSpec(memory_space=pl.ANY)
    dma = pltpu.SemaphoreType.DMA
    grad_hidden, grad_final, grad_scale, grad_shift = pl.pallas_call(
        kernel,
        out_shape=(
            jax.ShapeDtypeStruct((1, 64, 2432), BF16),
            jax.ShapeDtypeStruct((64, 76), F32),
            jax.ShapeDtypeStruct((1, 2432), F32),
            jax.ShapeDtypeStruct((1, 2432), F32),
        ),
        in_specs=[hbm] * 7,
        out_specs=(hbm,) * 4,
        scratch_shapes=[
            pltpu.VMEM((9, 16, 32), BF16),
            pltpu.VMEM((144, 16), BF16),
            pltpu.VMEM((1, 2432), F32),
            pltpu.VMEM((1, 2432), F32),
            pltpu.VMEM((64, 76), BF16),
            pltpu.VMEM((22, 128, 256), BF16),
            pltpu.VMEM((2, 64, 2432), BF16),
            pltpu.VMEM((8, 128, 256), BF16),
            pltpu.VMEM((16, 512), BF16),
            pltpu.VMEM((32, 16, 512), BF16),
            pltpu.VMEM((8, 21, 16, 128), BF16),
            pltpu.VMEM((640, 2304), BF16),
            pltpu.VMEM((2, 144, 128), F32),
            pltpu.VMEM((2304, 256), BF16),
            pltpu.VMEM((640, 256), F32),
            pltpu.VMEM((512, 128), F32),
            pltpu.VMEM((128, 128), F32),
            pltpu.VMEM((128, 128), F32),
            pltpu.VMEM((2, 4, 4, 48, 128), BF16),
            pltpu.VMEM((2440, 128), F32),
            pltpu.VMEM((2432, 128), BF16),
            pltpu.VMEM((128, 2432), F32),
            pltpu.VMEM((128, 128), F32),
            pltpu.VMEM((2448, 128), F32),
            pltpu.VMEM((1536, 128), BF16),
            pltpu.VMEM((128, 128), BF16),
            pltpu.VMEM((16, 48, 128), BF16),
            pltpu.VMEM((16, 48, 128), BF16),
            pltpu.VMEM((128, 2432), F32),
            pltpu.VMEM((64, 2432), BF16),
            pltpu.VMEM((64, 76), F32),
            pltpu.VMEM((1, 2432), F32),
            pltpu.VMEM((1, 2432), F32),
            pltpu.VMEM((2, 16, 128), F32),
            pltpu.VMEM((48, 128), BF16),
            pltpu.VMEM((16, 48, 128), BF16),
            dma((128,)),
            dma((8,)),
            dma, dma((8,)), dma, dma, dma,
            dma, dma, dma, dma,
            dma((4,)), dma((4,)), dma,
            dma, dma, dma, dma,
        ],
        compiler_params=pltpu.CompilerParams(
            collective_id=0, has_side_effects=True, vmem_limit_bytes=56 * 1024 * 1024
        ),
        cost_estimate=pl.CostEstimate(flops=1_000_000_000, bytes_accessed=2_000_000, transcendentals=0),
    )(
        grad_image,
        conv_weight.reshape(9, 16, 32),
        input_weight.reshape(144, 16),
        hidden,
        shift,
        scale,
        final_weight.T,
    )
    results = (grad_hidden, grad_final, grad_scale, grad_shift)
    grad_hidden, grad_final, grad_scale, grad_shift = pl.pallas_call(
        place,
        out_shape=tuple(jax.ShapeDtypeStruct(array.shape, array.dtype) for array in results),
        in_specs=[hbm] * 4,
        out_specs=(hbm,) * 4,
        scratch_shapes=[pltpu.VMEM(array.shape, array.dtype) for array in results] + [dma((14,))],
        compiler_params=pltpu.CompilerParams(vmem_limit_bytes=56 * 1024 * 1024),
    )(*results)
    return grad_hidden, grad_final.T, grad_scale, grad_shift


def solution(mesh):
    placed = (
        P("mem", "sp", None, None),
        P(None, None, "sp", "mem"),
        P(None, None, None, "sp"),
        P("mem", "sp", None),
        P("mem", None),
        P("mem", None),
        P("sp", None),
    )
    return jax.shard_map(
        per_device,
        mesh=mesh,
        in_specs=placed,
        out_specs=(P("mem", "sp", None), P("sp", None), P("mem", None), P("mem", None)),
        check_vma=False,
    )
```
